32 devices in a mesh: grp: 1, node: 32 (over z, y, x, core), dev: 1.
Axes of the slice: x: 2, y: 2, z: 4, core: 2. Of those that a mesh axis runs over, the one named last changes fastest.
Arguments:
- states: bfloat16 [256, 7168], P(('grp', 'node', 'dev')), may hold values from -6 to 6
- norm_gain: float32 [7168], replicated, may hold values from 0.1 to 1.9
- w_gate: bfloat16 [32, 7168, 512], P('node', None, 'dev'), may hold values from -0.0625 to 0.0625
- w_up: bfloat16 [32, 7168, 512], P('node', None, 'dev'), may hold values from -0.0625 to 0.0625
- w_down: bfloat16 [32, 512, 7168], P('node', 'dev'), may hold values from -0.125 to 0.125
- expert_ids: int32 [256, 2], P(('grp', 'node', 'dev')), may hold values from 0 to 7, all different within a row; in each aligned block of 8 rows (0 to 7, 8 to 15, ...) at most 4 rows name the same one
- route_weights: float32 [256, 2], P(('grp', 'node', 'dev')), may hold values from 0.5 to 2
- live_rows: int32 [256], P(('grp', 'node', 'dev')), may hold values 0 or 1
Outputs:
- mixed: bfloat16 [256, 7168], P(('grp', 'node', 'dev'))
The draws below stay inside these ranges and needn't reach their ends.
Inputs may be any that keep to these rules, and one draw needn't show every extreme that they name: `expert_ids`: each row names 2 different experts. Among the rows of one device (aligned blocks of 8 rows) no expert is named by more than 4 rows, and in every draw some expert is named by exactly 4 rows of some device.
All inputs are finite; a program needn't handle non-finite values. No bound on the sum of `live_rows` on one device may be relied on, other than what follows from the above.
Results may differ from the reference program's by a relative error of at most 0.0052.
Values may be sent and summed in bfloat16 or wider, within the bound.
A program may use at most 128 MiB of HBM per device.

```python
import math
import jax
import jax.numpy as jnp
import numpy as np
from jax import lax

D = 7168
HID = 2048
ROWS_DEV = 8
SPREAD = 4
TOP = 2
EXPERTS = 8
CAP = 4
ROWS = 256
N_NODE = 32


def with_ends(drawn, key, smallest, top_value):
    longest = drawn.shape.index(max(drawn.shape))
    spots = []
    for shift in (0, 1):
        where = [jax.random.randint(jax.random.fold_in(key, axis), (), 0, length) for axis, length in enumerate(drawn.shape)]
        where[longest] = (where[longest] + shift) % drawn.shape[longest]
        spots.append(tuple(where))
    return drawn.at[spots[0]].set(smallest).at[spots[1]].set(top_value)


def shard_levels(rng, shape, pieces, smallest, top_value):
    def one(position, shards_of):
        heights = jax.random.uniform(jax.random.fold_in(jax.random.fold_in(rng, 6), position), (shards_of,), jnp.float32, smallest / len(pieces), top_value / len(pieces))
        return jnp.repeat(jnp.exp(heights), shape[position] // shards_of).reshape((-1,) + (1,) * (len(shape) - position - 1))

    level = one(*pieces[0])
    for cut in pieces[1:]:
        level = level * one(*cut)
    return level


def deal_out(own_key, own, number, rows, count, top, limit, slope):
    ranking = jax.random.permutation(own_key, count)
    crowded, common = load_shares(count, rows * top, limit, slope, True), load_shares(count, rows * top, limit, slope, False)
    places = jnp.arange(count)

    def named(sizes, offset_by):
        used = int((sizes > 0).sum())
        fixed = max(1, used // 4)
        shifted = fixed + (places - fixed + offset_by * (used - fixed)) % max(1, count - fixed)
        return jnp.zeros((count,), jnp.int32).at[ranking[jnp.where(places < fixed, places, shifted)]].set(jnp.asarray(sizes, jnp.int32))

    sizes = jnp.where(number % 4 == 0, named(crowded, number // 4), named(common, number - number // 4 - 1))
    mixed = jax.random.permutation(jax.random.fold_in(own, 3), count)
    giver, taker = mixed[0:count // 2 * 2:2], mixed[1:count // 2 * 2:2]
    slack = jnp.minimum(sizes[giver] - 1, limit - sizes[taker]) // 2
    slack = jnp.where((giver == ranking[0]) | (taker == ranking[0]) | (sizes[taker] == 0), 0, jnp.maximum(slack, 0))
    shifted = jax.random.randint(jax.random.fold_in(own, 4), (count // 2,), 0, 1 << 20) % (slack + 1)
    sizes = sizes.at[giver].add(-shifted).at[taker].add(shifted)
    labels = jnp.searchsorted(jnp.cumsum(sizes), jnp.arange(rows * top), side="right").astype(jnp.int32)
    table = labels.reshape(top, rows).T
    table = table[jax.random.permutation(jax.random.fold_in(own, 1), rows)]
    offset_by = jax.random.randint(jax.random.fold_in(own, 2), (rows, 1), 0, top)
    return jnp.take_along_axis(table, (jnp.arange(top)[None, :] + offset_by) % top, axis=1)


def load_shares(amount, total, reach, skew, full):
    portions = [(1 << 20) // math.isqrt(standing ** skew) + 1 for standing in range(1, amount + 1)]
    largest = reach if full else min(reach, max(-(-total // amount), total * portions[0] // sum(portions)))
    least = 1 if total - largest >= amount - 1 else 0
    counts, surplus = [largest] + [least] * (amount - 1), total - largest - least * (amount - 1)
    while surplus > 0:
        candidates = [i for i in range(1, amount) if counts[i] < largest] or [i for i in range(1, amount) if counts[i] < reach]
        whole, budget = sum([portions[i] for i in candidates]), surplus
        for i in candidates:
            addition = min(reach - counts[i], max(1, budget * portions[i] // whole), surplus)
            counts[i] = counts[i] + addition
            surplus = surplus - addition
    return np.array(counts)


def centred(key, extent, deviation, bound, pieces=(), kind=jnp.bfloat16):
    array = jax.random.normal(key, extent, jnp.float32) * deviation
    if len(pieces) > 0:
        array = shard_levels(key, extent, pieces, -0.22, 0.18) * array
    return jnp.clip(array, min=-bound, max=bound).astype(kind)


def setup_inputs(seed: int = 0, part: int = 0) -> dict:
    splits = jax.random.split(jax.random.key(seed), 9)
    own_keys = jax.random.split(jax.random.fold_in(splits[8], part), 9)
    states = centred(own_keys[0], (ROWS, D), 1.0, 6.0, ((0, 32),))
    norm_gain = jnp.clip(1.0 + 0.18 * jax.random.normal(splits[1], (D,), jnp.float32), 0.1, 1.9)
    w_gate = centred(splits[2], (N_NODE, D, HID // SPREAD), D ** -0.5, 0.0625, ((0, 32),))
    w_up = centred(splits[3], (N_NODE, D, HID // SPREAD), D ** -0.5, 0.0625, ((0, 32),))
    w_down = centred(splits[4], (N_NODE, HID // SPREAD, D), HID ** -0.5, 0.125, ((0, 32),))
    expert_ids_keys = jax.random.split(jax.random.fold_in(own_keys[5], 1), ROWS // ROWS_DEV)
    expert_ids_turns = jax.random.permutation(jax.random.fold_in(own_keys[5], 3), ROWS // ROWS_DEV)
    expert_ids = jax.vmap(lambda own, number: deal_out(jax.random.fold_in(own_keys[5], 2), own, number, ROWS_DEV, EXPERTS, TOP, CAP, 2))(expert_ids_keys, expert_ids_turns).reshape((ROWS, TOP))
    route_weights = jnp.clip(0.5 + 1.5 * jax.random.uniform(own_keys[6], (ROWS, TOP), jnp.float32) ** shard_levels(own_keys[6], (ROWS, TOP), ((0, 32),), -0.2, 0.2), 0.5, 2.0)
    live_rows = with_ends((jax.random.randint(own_keys[7], (ROWS,), 0, 4) < 3).astype(jnp.int32), jax.random.fold_in(own_keys[7], 1), 0, 1)
    return {"states": states, "norm_gain": norm_gain, "w_gate": w_gate, "w_up": w_up, "w_down": w_down, "expert_ids": expert_ids, "route_weights": route_weights, "live_rows": live_rows}


norm_eps = 1e-06

def reference(states, norm_gain, w_gate, w_up, w_down, expert_ids, route_weights, live_rows):
    states_float = states.astype(jnp.float32)
    mean_square = lax.optimization_barrier(jnp.mean(states_float * states_float, axis=1, keepdims=True))
    normed = (states_float * lax.rsqrt(mean_square + norm_eps) * norm_gain).astype(jnp.bfloat16)

    def add_expert(running, expert_index):
        first_block = (expert_index * SPREAD).astype(jnp.int32)
        gate_block = lax.dynamic_slice_in_dim(w_gate, first_block, SPREAD, 0)
        up_block = lax.dynamic_slice_in_dim(w_up, first_block, SPREAD, 0)
        down_block = lax.dynamic_slice_in_dim(w_down, first_block, SPREAD, 0)
        gate_full = jnp.transpose(gate_block, (1, 0, 2)).reshape(D, HID)
        up_full = jnp.transpose(up_block, (1, 0, 2)).reshape(D, HID)
        down_full = down_block.reshape(HID, D)
        gate = jnp.dot(normed, gate_full, preferred_element_type=jnp.float32)
        up_value = jnp.dot(normed, up_full, preferred_element_type=jnp.float32)
        hidden = (jax.nn.silu(gate) * up_value).astype(jnp.bfloat16)
        expert_out = jnp.dot(hidden, down_full, preferred_element_type=jnp.float32)
        weight = lax.optimization_barrier(jnp.sum(jnp.where(expert_ids == expert_index, route_weights, jnp.zeros_like(route_weights)), axis=1))
        return (running + weight[:, None] * expert_out, None)
    start_sum = jnp.zeros((states.shape[0], D), jnp.float32)
    branch_sum, unused = lax.scan(add_expert, start_sum, jnp.arange(EXPERTS, dtype=jnp.int32))
    return (states_float + live_rows[:, None].astype(jnp.float32) * branch_sum).astype(jnp.bfloat16)
```

```python
import functools

import jax
import jax.numpy as jnp
from jax import lax
from jax.experimental import pallas as pl
from jax.experimental.pallas import tpu as pltpu
from jax.sharding import PartitionSpec as P

SPREAD = 4
norm_eps = 1e-06
F32 = jnp.float32
BF16 = jnp.bfloat16


def flip(value, bit):
    return value + bit - 2 * bit * ((value // bit) % 2)


def xor(value, mask):
    bit = 1
    while bit <= mask:
        if mask & bit:
            value = flip(value, bit)
        bit *= 2
    return value


def kernel(E, M, DEVC, states, gain, w_gate, w_up, w_down, ids, route, live, out,
           wg, wu, wd, s0, g0, s1, X, acc, send_r, recv_r, fin, ret, s4, g4,
           w_sem, s0_sem, s1_sem, s2_sem, r_sem, f_sem, s4_sem):
    rows, width = states.shape
    cols = width // M
    S = s1.shape[1]
    cap = S // M
    bits = []
    b = 1
    while b < M:
        bits.append(b)
        b *= 2
    grp = lax.axis_index("grp")
    node = lax.axis_index("node")
    dev = lax.axis_index("dev")
    g = node // SPREAD
    m = (node % SPREAD) * DEVC + dev

    def device(group, member):
        return (grp, group * SPREAD + member // DEVC, member % DEVC)

    def remote(src, dst, sems, at, target):
        return pltpu.make_async_remote_copy(
            src_ref=src, dst_ref=dst, send_sem=sems.at[0, at], recv_sem=sems.at[1, at],
            device_id=target, device_id_type=pl.DeviceIdType.MESH)

    w_copies = {}
    for r in range(M):
        j = xor(m, r)
        span = pl.ds(pl.multiple_of(j * cols, cols), cols)
        w_copies[0, r] = pltpu.make_async_copy(w_gate.at[0, span, :], wg.at[j], w_sem.at[0, r])
        w_copies[1, r] = pltpu.make_async_copy(w_up.at[0, span, :], wu.at[j], w_sem.at[1, r])
        w_copies[2, r] = pltpu.make_async_copy(w_down.at[0, :, span], wd.at[j], w_sem.at[2, r])
    for r in range(M):
        w_copies[0, r].start()
        w_copies[1, r].start()
    for r in reversed(range(M)):
        w_copies[2, r].start()

    barrier = pltpu.get_barrier_semaphore()
    for r in range(1, M):
        pl.semaphore_signal(barrier, inc=1, device_id=device(g, xor(m, r)),
                            device_id_type=pl.DeviceIdType.MESH)
    for k in range(1, E):
        pl.semaphore_signal(barrier, inc=1, device_id=device((g + k) % E, m),
                            device_id_type=pl.DeviceIdType.MESH)

    x = states[...].astype(F32)
    mean_square = jnp.mean(x * x, axis=1, keepdims=True)
    normed = (x * lax.rsqrt(mean_square + norm_eps) * gain[...]).astype(BF16).astype(F32)
    lane = lax.broadcasted_iota(jnp.int32, (rows, E * S), 1)
    row = lax.broadcasted_iota(jnp.int32, (rows, E * S), 0)
    expert = lane // S
    hit_weight = jnp.zeros((rows, E * S), F32)
    hit = jnp.zeros((rows, E * S), jnp.int32)
    for k in range(ids.shape[1]):
        here = ids[:, k:k + 1] == expert
        hit = hit + here.astype(jnp.int32)
        hit_weight = hit_weight + jnp.where(here, route[:, k:k + 1], 0.0)
    rank = jnp.zeros((rows, E * S), jnp.int32)
    for r in range(rows - 1):
        rank = rank + jnp.where(row > r, hit[r:r + 1, :], 0)
    placed = jnp.where(rank + m * cap == lane % S, hit_weight, 0.0)
    for j in range(M):
        s0[j, :, :cols] = normed[:, j * cols:(j + 1) * cols]
        s0[j, :, cols:] = placed

    pl.semaphore_wait(barrier, M - 1 + E - 1)

    c0 = []
    for r in reversed(range(1, M)):
        p = xor(m, r)
        c = remote(s0.at[p], g0.at[m], s0_sem, r, device(g, p))
        c.start()
        c0.append(c)
    g0[m] = s0[m]
    for c in c0:
        c.wait()
    place = g0[:, :, cols:].reshape(M * rows, E * S)
    mine = g0[:, :, :cols].reshape(M * rows, cols).astype(BF16)
    onehot = jnp.where(place > 0, 1.0, 0.0).T.astype(BF16)
    packed = jnp.dot(onehot, mine, preferred_element_type=F32).astype(BF16)
    s1[...] = packed.reshape(E, S, cols)

    c1 = []
    for k in range(1, E):
        e = (g + k) % E
        c = remote(s1.at[e], X.at[m, g], s1_sem, k, device(e, m))
        c.start()
        c1.append(c)
    X[m, g] = s1[g]
    order = [(g + E - k) % E for k in range(E)]
    c2 = {}

    def forward(block, r, bit):
        j = xor(m, r)
        c = remote(X.at[j, block[1]], X.at[j, block[1]], s2_sem, (r + bit) * E + block[0],
                   device(g, flip(m, bit)))
        c.start()
        c2[r + bit, block[0]] = c

    for k in range(E):
        if k:
            c1[k - 1].wait()
        for bit in reversed(bits):
            forward((k, order[k]), 0, bit)
    for r in sorted(range(1, M), key=lambda v: bin(v).count("1")):
        low = r & -r
        if low > 1:
            for k in range(E):
                c2[r, k].wait_recv()
                for bit in reversed(bits):
                    if bit < low:
                        forward((k, order[k]), r, bit)

    hid = wg.shape[2]
    gate = jnp.zeros((E * S, hid), F32)
    up = jnp.zeros((E * S, hid), F32)
    for r in range(M):
        j = xor(m, r)
        w_copies[0, r].wait()
        w_copies[1, r].wait()
        if r & 1:
            for k in range(E):
                c2[r, k].wait_recv()
        xs = X[j].reshape(E * S, cols)
        gate = gate + jnp.dot(xs, wg[j], preferred_element_type=F32)
        up = up + jnp.dot(xs, wu[j], preferred_element_type=F32)
    hidden = (gate / (1.0 + jnp.exp(-gate)) * up).astype(BF16)

    back = [(g + k + 1) % E for k in range(E)]
    cr = {}
    cf = []
    for r in reversed(range(M)):
        j = xor(m, r)
        w_copies[2, r].wait()
        part = jnp.dot(hidden, wd[j], preferred_element_type=F32)
        low = r & -r
        if low == 1:
            send_r[r - 1] = part.astype(BF16).reshape(E, S, cols)
        else:
            acc[...] = part.reshape(E, S, cols)
        for k in range(E):
            e = back[k]
            if low != 1:
                total = acc[e]
                for bit in bits:
                    if r & bit:
                        break
                    cr[r + bit, k].wait_recv()
                    total = total + recv_r[r + bit - 1, e].astype(F32)
                if r:
                    send_r[r - 1, e] = total.astype(BF16)
                else:
                    fin[e] = total.astype(BF16)
            if r:
                c = remote(send_r.at[r - 1, e], recv_r.at[r - 1, e], r_sem, r * E + k,
                           device(g, flip(m, low)))
                c.start()
                cr[r, k] = c
            elif k < E - 1:
                c = remote(fin.at[e], ret.at[g], f_sem, k, device(e, m))
                c.start()
                cf.append(c)
    ret[g] = fin[g]
    for c in cf:
        c.wait()
    place = g0[:, :, cols:].reshape(M * rows, E * S)
    high = place.astype(BF16)
    rest = (place - high.astype(F32)).astype(BF16)
    got = ret[...].reshape(E * S, cols)
    branch = (jnp.dot(high, got, preferred_element_type=F32)
              + jnp.dot(rest, got, preferred_element_type=F32))
    s4[...] = branch.reshape(M, rows, cols)
    c4 = []
    for r in reversed(range(1, M)):
        p = xor(m, r)
        c = remote(s4.at[p], g4.at[m], s4_sem, r, device(g, p))
        c.start()
        c4.append(c)
    g4[m] = s4[m]
    for c in c4:
        c.wait()
    for j in range(M):
        span = slice(j * cols, (j + 1) * cols)
        out[:, span] = (states[:, span].astype(F32) + live[...] * g4[j]).astype(BF16)
    for c in list(c2.values()) + list(cr.values()):
        c.wait_send()


def body(states, norm_gain, w_gate, w_up, w_down, expert_ids, route_weights, live_rows):
    rows, width = states.shape
    nodes = lax.axis_size("node")
    devc = lax.axis_size("dev")
    E = nodes // SPREAD
    M = SPREAD * devc
    cap = min(rows, rows * expert_ids.shape[1] // E * 2)
    S = cap * M
    cols = width // M
    hid = w_gate.shape[2]
    vmem = pl.BlockSpec(memory_space=pltpu.VMEM)
    hbm = pl.BlockSpec(memory_space=pl.ANY)
    dma = pltpu.SemaphoreType.DMA
    return pl.pallas_call(
        functools.partial(kernel, E, M, devc),
        out_shape=jax.ShapeDtypeStruct((rows, width), BF16),
        in_specs=[vmem, vmem, hbm, hbm, hbm, vmem, vmem, vmem],
        out_specs=vmem,
        scratch_shapes=[
            pltpu.VMEM((M, cols, hid), BF16),
            pltpu.VMEM((M, cols, hid), BF16),
            pltpu.VMEM((M, hid, cols), BF16),
            pltpu.VMEM((M, rows, cols + E * S), F32),
            pltpu.VMEM((M, rows, cols + E * S), F32),
            pltpu.VMEM((E, S, cols), BF16),
            pltpu.VMEM((M, E, S, cols), BF16),
            pltpu.VMEM((E, S, cols), F32),
            pltpu.VMEM((M - 1, E, S, cols), BF16),
            pltpu.VMEM((M - 1, E, S, cols), BF16),
            pltpu.VMEM((E, S, cols), BF16),
            pltpu.VMEM((E, S, cols), BF16),
            pltpu.VMEM((M, rows, cols), F32),
            pltpu.VMEM((M, rows, cols), F32),
            dma((3, M)), dma((2, M)), dma((2, E)), dma((2, M * E)), dma((2, M * E)),
            dma((2, E)), dma((2, M)),
        ],
        compiler_params=pltpu.CompilerParams(
            collective_id=0, has_side_effects=True, vmem_limit_bytes=56 * 1024 * 1024),
    )(states, norm_gain.reshape(1, width), w_gate, w_up, w_down, expert_ids, route_weights,
      live_rows.reshape(rows, 1).astype(F32))


def solution(mesh):
    placed = (
        P(("grp", "node", "dev"), None),
        P(),
        P("node", None, "dev"),
        P("node", None, "dev"),
        P("node", "dev", None),
        P(("grp", "node", "dev"), None),
        P(("grp", "node", "dev"), None),
        P(("grp", "node", "dev")),
    )
    return jax.shard_map(
        body, mesh=mesh, in_specs=placed, out_specs=P(("grp", "node", "dev"), None), check_vma=False
    )
```

```python
import functools

import jax
import jax.numpy as jnp
from jax import lax
from jax.experimental import pallas as pl
from jax.experimental.pallas import tpu as pltpu
from jax.sharding import PartitionSpec as P

SPREAD = 4
norm_eps = 1e-06
F32 = jnp.float32
BF16 = jnp.bfloat16


def flip(value, bit):
    return value + bit - 2 * bit * ((value // bit) % 2)


def xor(value, mask):
    bit = 1
    while bit <= mask:
        if mask & bit:
            value = flip(value, bit)
        bit *= 2
    return value


def fold(value, half):
    rows, cols = value.shape
    second = value[:, half:]
    if cols < 2 * half:
        second = jnp.concatenate([second, jnp.zeros((rows, 2 * half - cols), F32)], axis=1)
    return jnp.concatenate([value[:, :half], second], axis=0)


def unfold(value, cols):
    rows, half = value.shape[0] // 2, value.shape[1]
    return jnp.concatenate([value[:rows], value[rows:, :cols - half]], axis=1)


def far_first(E):
    return list(range(E - 1, 0, -1))


def kernel(E, M, DEVC, states, gain, w_gate, w_up, w_down, ids, route, live, out,
           wg, wu, wd, s0, g0, s1, X, acc, send_r, recv_r, fin, ret, s4, g4,
           w_sem, s0_sem, s1_sem, s2_sem, r_sem, f_sem, s4_sem):
    rows, width = states.shape
    cols = width // M
    S = s1.shape[1]
    cap = S // M
    half = s4.shape[2]
    bits = []
    b = 1
    while b < M:
        bits.append(b)
        b *= 2
    grp = lax.axis_index("grp")
    node = lax.axis_index("node")
    dev = lax.axis_index("dev")
    g = node // SPREAD
    m = (node % SPREAD) * DEVC + dev

    def device(group, member):
        return (grp, group * SPREAD + member // DEVC, member % DEVC)

    def remote(src, dst, sems, at, target):
        return pltpu.make_async_remote_copy(
            src_ref=src, dst_ref=dst, send_sem=sems.at[0, at], recv_sem=sems.at[1, at],
            device_id=target, device_id_type=pl.DeviceIdType.MESH)

    w_copies = {}
    for r in range(M):
        j = xor(m, r)
        span = pl.ds(pl.multiple_of(j * cols, cols), cols)
        w_copies[0, r] = pltpu.make_async_copy(w_gate.at[0, span, :], wg.at[j], w_sem.at[0, r])
        w_copies[1, r] = pltpu.make_async_copy(w_up.at[0, span, :], wu.at[j], w_sem.at[1, r])
        w_copies[2, r] = pltpu.make_async_copy(w_down.at[0, :, span], wd.at[j], w_sem.at[2, r])
    for r in range(M):
        w_copies[0, r].start()
        w_copies[1, r].start()
    for r in reversed(range(M)):
        w_copies[2, r].start()

    barrier = pltpu.get_barrier_semaphore()
    for r in range(1, M):
        pl.semaphore_signal(barrier, inc=1, device_id=device(g, xor(m, r)),
                            device_id_type=pl.DeviceIdType.MESH)
    for k in range(1, E):
        pl.semaphore_signal(barrier, inc=1, device_id=device(xor(g, k), m),
                            device_id_type=pl.DeviceIdType.MESH)

    x = states[...].astype(F32)
    mean_square = jnp.mean(x * x, axis=1, keepdims=True)
    normed = (x * lax.rsqrt(mean_square + norm_eps) * gain[...]).astype(BF16).astype(F32)
    lane = lax.broadcasted_iota(jnp.int32, (rows, E * S), 1)
    row = lax.broadcasted_iota(jnp.int32, (rows, E * S), 0)
    expert = (lane // S).astype(F32)
    diagonal = (lax.broadcasted_iota(jnp.int32, (rows, rows), 0)
                == lax.broadcasted_iota(jnp.int32, (rows, rows), 1))

    def column(line):
        spread = jnp.broadcast_to(line.astype(F32), (rows, rows))
        return jnp.sum(jnp.where(diagonal, spread, 0.0), axis=1, keepdims=True)

    hit_weight = jnp.zeros((rows, E * S), F32)
    hit = jnp.zeros((rows, E * S), jnp.int32)
    for k in range(ids.shape[0]):
        here = column(ids[k:k + 1, :]) == expert
        hit = hit + here.astype(jnp.int32)
        hit_weight = hit_weight + jnp.where(here, column(route[k:k + 1, :]), 0.0)
    rank = jnp.zeros((rows, E * S), jnp.int32)
    for r in range(rows - 1):
        rank = rank + jnp.where(row > r, hit[r:r + 1, :], 0)
    placed = jnp.where(rank + m * cap == lane % S, hit_weight, 0.0)
    high = placed.astype(BF16).astype(F32)
    for j in range(M):
        s0[j, :, :half] = fold(normed[:, j * cols:(j + 1) * cols], half).astype(BF16)
        s0[j, :, half:] = jnp.concatenate([high, placed - high], axis=0).astype(BF16)

    pl.semaphore_wait(barrier, M - 1 + E - 1)

    c0 = []
    for r in reversed(range(1, M)):
        p = xor(m, r)
        c = remote(s0.at[p], g0.at[m], s0_sem, r, device(g, p))
        c.start()
        c0.append(c)
    g0[m] = s0[m]
    for c in c0:
        c.wait()
    got = [g0[r].astype(F32) for r in range(M)]
    high = jnp.concatenate([v[:rows, half:] for v in got], axis=0)
    rest = jnp.concatenate([v[rows:, half:] for v in got], axis=0)
    place = high + rest
    mine = jnp.concatenate([unfold(v[:, :half], cols) for v in got], axis=0).astype(BF16)
    onehot = jnp.where(place > 0, 1.0, 0.0).T.astype(BF16)
    packed = jnp.dot(onehot, mine, preferred_element_type=F32).astype(BF16)
    s1[...] = packed.reshape(E, S, cols)

    c1 = {}
    for k in far_first(E):
        e = xor(g, k)
        c = remote(s1.at[e], X.at[m, g], s1_sem, k, device(e, m))
        c.start()
        c1[k] = c
    X[m, g] = s1[g]
    order = [xor(g, k) for k in range(E)]
    c2 = {}

    def forward(block, r, bit):
        j = xor(m, r)
        c = remote(X.at[j, block[1]], X.at[j, block[1]], s2_sem, (r + bit) * E + block[0],
                   device(g, flip(m, bit)))
        c.start()
        c2[r + bit, block[0]] = c

    for k in range(E):
        if k:
            c1[k].wait_recv()
        for bit in reversed(bits):
            forward((k, order[k]), 0, bit)
    hid = wg.shape[2]
    gate = jnp.zeros((E * S, hid), F32)
    up = jnp.zeros((E * S, hid), F32)
    for r in range(M):
        j = xor(m, r)
        w_copies[0, r].wait()
        w_copies[1, r].wait()
        for k in range(E if r else 0):
            c2[r, k].wait_recv()
            for bit in reversed(bits):
                if bit < (r & -r):
                    forward((k, order[k]), r, bit)
        xs = X[j].reshape(E * S, cols)
        gate = gate + jnp.dot(xs, wg[j], preferred_element_type=F32)
        up = up + jnp.dot(xs, wu[j], preferred_element_type=F32)
    hidden = (gate / (1.0 + jnp.exp(-gate)) * up).astype(BF16)

    turns = far_first(E) + [0]
    back = [xor(g, k) for k in turns]
    cr = {}
    cf = []
    for r in reversed(range(M)):
        j = xor(m, r)
        w_copies[2, r].wait()
        part = jnp.dot(hidden, wd[j], preferred_element_type=F32)
        low = r & -r
        if low == 1:
            send_r[r - 1] = part.astype(BF16).reshape(E, S, cols)
        else:
            acc[...] = part.reshape(E, S, cols)
        for k in range(E):
            e = back[k]
            if low != 1:
                total = acc[e]
                for bit in bits:
                    if r & bit:
                        break
                    cr[r + bit, k].wait_recv()
                    total = total + recv_r[r + bit - 1, e].astype(F32)
                if r:
                    send_r[r - 1, e] = total.astype(BF16)
                else:
                    fin[e] = total.astype(BF16)
            if r:
                c = remote(send_r.at[r - 1, e], recv_r.at[r - 1, e], r_sem, r * E + k,
                           device(g, flip(m, low)))
                c.start()
                cr[r, k] = c
            elif k < E - 1:
                c = remote(fin.at[e], ret.at[g], f_sem, turns[k], device(e, m))
                c.start()
                cf.append(c)
    ret[g] = fin[g]
    for c in cf:
        c.wait()
    high = high.astype(BF16)
    rest = rest.astype(BF16)
    got = ret[...].reshape(E * S, cols)
    branch = (jnp.dot(high, got, preferred_element_type=F32)
              + jnp.dot(rest, got, preferred_element_type=F32))
    for j in range(M):
        s4[j] = fold(branch[j * rows:(j + 1) * rows], half).astype(BF16)
    c4 = []
    for r in reversed(range(1, M)):
        p = xor(m, r)
        c = remote(s4.at[p], g4.at[m], s4_sem, r, device(g, p))
        c.start()
        c4.append(c)
    g4[m] = s4[m]
    for c in c4:
        c.wait()
    alive = column(live[...])
    for j in range(M):
        span = slice(j * cols, (j + 1) * cols)
        out[:, span] = (states[:, span].astype(F32) + alive * unfold(g4[j].astype(F32), cols)).astype(BF16)
    for c in list(c1.values()) + list(c2.values()) + list(cr.values()):
        c.wait_send()


def body(states, norm_gain, w_gate, w_up, w_down, expert_ids, route_weights, live_rows):
    rows, width = states.shape
    nodes = lax.axis_size("node")
    devc = lax.axis_size("dev")
    E = nodes // SPREAD
    M = SPREAD * devc
    cap = min(rows, rows * expert_ids.shape[1] // E * 2)
    S = cap * M
    cols = width // M
    half = -(-cols // 256) * 128
    hid = w_gate.shape[2]
    vmem = pl.BlockSpec(memory_space=pltpu.VMEM)
    hbm = pl.BlockSpec(memory_space=pl.ANY)
    dma = pltpu.SemaphoreType.DMA
    return pl.pallas_call(
        functools.partial(kernel, E, M, devc),
        out_shape=jax.ShapeDtypeStruct((rows, width), BF16),
        in_specs=[vmem, vmem, hbm, hbm, hbm, vmem, vmem, vmem],
        out_specs=vmem,
        scratch_shapes=[
            pltpu.VMEM((M, cols, hid), BF16),
            pltpu.VMEM((M, cols, hid), BF16),
            pltpu.VMEM((M, hid, cols), BF16),
            pltpu.VMEM((M, 2 * rows, half + E * S), BF16),
            pltpu.VMEM((M, 2 * rows, half + E * S), BF16),
            pltpu.VMEM((E, S, cols), BF16),
            pltpu.VMEM((M, E, S, cols), BF16),
            pltpu.VMEM((E, S, cols), F32),
            pltpu.VMEM((M - 1, E, S, cols), BF16),
            pltpu.VMEM((M - 1, E, S, cols), BF16),
            pltpu.VMEM((E, S, cols), BF16),
            pltpu.VMEM((E, S, cols), BF16),
            pltpu.VMEM((M, 2 * rows, half), BF16),
            pltpu.VMEM((M, 2 * rows, half), BF16),
            dma((3, M)), dma((2, M)), dma((2, E)), dma((2, M * E)), dma((2, M * E)),
            dma((2, E)), dma((2, M)),
        ],
        compiler_params=pltpu.CompilerParams(
            collective_id=0, has_side_effects=True, vmem_limit_bytes=56 * 1024 * 1024),
    )(states, norm_gain.reshape(1, width), w_gate, w_up, w_down, expert_ids.T, route_weights.T,
      live_rows.reshape(1, rows))


def solution(mesh):
    placed = (
        P(("grp", "node", "dev"), None),
        P(),
        P("node", None, "dev"),
        P("node", None, "dev"),
        P("node", "dev", None),
        P(("grp", "node", "dev"), None),
        P(("grp", "node", "dev"), None),
        P(("grp", "node", "dev")),
    )
    return jax.shard_map(
        body, mesh=mesh, in_specs=placed, out_specs=P(("grp", "node", "dev"), None), check_vma=False
    )
```

```python
import functools

import jax
import jax.numpy as jnp
from jax import lax
from jax.experimental import pallas as pl
from jax.experimental.pallas import tpu as pltpu
from jax.sharding import PartitionSpec as P

SPREAD = 4
W = 4
V = 2
norm_eps = 1e-06
F32 = jnp.float32
BF16 = jnp.bfloat16


def flip(value, bit):
    return value + bit - 2 * bit * ((value // bit) % 2)


def xor(value, mask):
    bit = 1
    while bit <= mask:
        if mask & bit:
            value = flip(value, bit)
        bit *= 2
    return value


def fold(value, half):
    rows, cols = value.shape
    second = value[:, half:]
    if cols < 2 * half:
        second = jnp.concatenate([second, jnp.zeros((rows, 2 * half - cols), F32)], axis=1)
    return jnp.concatenate([value[:, :half], second], axis=0)


def unfold(value, cols):
    rows, half = value.shape[0] // 2, value.shape[1]
    return jnp.concatenate([value[:rows], value[rows:, :cols - half]], axis=1)


def far_first(E):
    return list(range(E - 1, 0, -1))


def kernel(E, M, DEVC, states, gain, w_gate, w_up, w_down, ids, route, live, out,
           wg, wu, wd, s0, g0, s1, X, acc, send_r, recv_r, fin, ret, s4, g4,
           w_sem, s0_sem, s1_sem, s2_sem, r_sem, f_sem, s4_sem):
    rows, width = states.shape
    cols = width // M
    S = s1.shape[1]
    cap = S // M
    half = s4.shape[2]
    bits = []
    b = 1
    while b < M:
        bits.append(b)
        b *= 2
    grp = lax.axis_index("grp")
    node = lax.axis_index("node")
    dev = lax.axis_index("dev")
    g = node // SPREAD
    m = (node % SPREAD) * DEVC + dev

    def device(group, member):
        return (grp, group * SPREAD + member // DEVC, member % DEVC)

    def remote(src, dst, sems, at, target):
        return pltpu.make_async_remote_copy(
            src_ref=src, dst_ref=dst, send_sem=sems.at[0, at], recv_sem=sems.at[1, at],
            device_id=target, device_id_type=pl.DeviceIdType.MESH)

    w_copies = {}
    for r in range(M):
        j = xor(m, r)
        span = pl.ds(pl.multiple_of(j * cols, cols), cols)
        w_copies[0, r] = pltpu.make_async_copy(w_gate.at[0, span, :], wg.at[j], w_sem.at[0, r])
        w_copies[1, r] = pltpu.make_async_copy(w_up.at[0, span, :], wu.at[j], w_sem.at[1, r])
        w_copies[2, r] = pltpu.make_async_copy(w_down.at[0, :, span], wd.at[j], w_sem.at[2, r])
    for r in range(M):
        w_copies[0, r].start()
        w_copies[1, r].start()
    for r in reversed(range(M)):
        w_copies[2, r].start()

    barrier = pltpu.get_barrier_semaphore()
    for r in range(1, M):
        pl.semaphore_signal(barrier, inc=1, device_id=device(g, xor(m, r)),
                            device_id_type=pl.DeviceIdType.MESH)
    for k in range(1, E):
        pl.semaphore_signal(barrier, inc=1, device_id=device(xor(g, k), m),
                            device_id_type=pl.DeviceIdType.MESH)

    x = states[...].astype(F32)
    mean_square = jnp.mean(x * x, axis=1, keepdims=True)
    normed = (x * lax.rsqrt(mean_square + norm_eps) * gain[...]).astype(BF16).astype(F32)
    lane = lax.broadcasted_iota(jnp.int32, (rows, E * S), 1)
    row = lax.broadcasted_iota(jnp.int32, (rows, E * S), 0)
    expert = (lane // S).astype(F32)
    diagonal = (lax.broadcasted_iota(jnp.int32, (rows, rows), 0)
                == lax.broadcasted_iota(jnp.int32, (rows, rows), 1))

    def column(line):
        spread = jnp.broadcast_to(line.astype(F32), (rows, rows))
        return jnp.sum(jnp.where(diagonal, spread, 0.0), axis=1, keepdims=True)

    hit_weight = jnp.zeros((rows, E * S), F32)
    hit = jnp.zeros((rows, E * S), jnp.int32)
    for k in range(ids.shape[0]):
        here = column(ids[k:k + 1, :]) == expert
        hit = hit + here.astype(jnp.int32)
        hit_weight = hit_weight + jnp.where(here, column(route[k:k + 1, :]), 0.0)
    rank = jnp.zeros((rows, E * S), jnp.int32)
    for r in range(rows - 1):
        rank = rank + jnp.where(row > r, hit[r:r + 1, :], 0)
    placed = jnp.where(rank + m * cap == lane % S, hit_weight, 0.0)
    high = placed.astype(BF16).astype(F32)
    for j in range(M):
        s0[j, :, :half] = fold(normed[:, j * cols:(j + 1) * cols], half).astype(BF16)
        s0[j, :, half:] = jnp.concatenate([high, placed - high], axis=0).astype(BF16)

    pl.semaphore_wait(barrier, M - 1 + E - 1)

    c0 = []
    for r in reversed(range(1, M)):
        p = xor(m, r)
        c = remote(s0.at[p], g0.at[m], s0_sem, r, device(g, p))
        c.start()
        c0.append(c)
    g0[m] = s0[m]
    for c in c0:
        c.wait()
    got = [g0[r].astype(F32) for r in range(M)]
    high = jnp.concatenate([v[:rows, half:] for v in got], axis=0)
    rest = jnp.concatenate([v[rows:, half:] for v in got], axis=0)
    place = high + rest
    mine = jnp.concatenate([unfold(v[:, :half], cols) for v in got], axis=0).astype(BF16)
    onehot = jnp.where(place > 0, 1.0, 0.0).T.astype(BF16)
    packed = jnp.dot(onehot, mine, preferred_element_type=F32).astype(BF16)
    s1[...] = packed.reshape(E, S, cols)

    c1 = {}
    for k in list(range(E // 2, E)) + list(range(1, E // 2)):
        e = xor(g, k)
        c = remote(s1.at[e], X.at[m, g], s1_sem, k, device(e, m))
        if k < E // 2 + V:
            c.start()
        c1[k] = c
    X[m, g] = s1[g]
    order = [xor(g, k) for k in range(E)]
    c2 = {}

    def forward(block, r, bit):
        j = xor(m, r)
        c = remote(X.at[j, block[1]], X.at[j, block[1]], s2_sem, (r + bit) * E + block[0],
                   device(g, flip(m, bit)))
        c.start()
        c2[r + bit, block[0]] = c

    for k in range(E):
        if k:
            c1[k].wait_recv()
        if k >= E // 2 and k + V < E:
            c1[k].wait_send()
            c1[k + V].start()
        for bit in reversed(bits):
            forward((k, order[k]), 0, bit)
    hid = wg.shape[2]
    gate = jnp.zeros((E * S, hid), F32)
    up = jnp.zeros((E * S, hid), F32)
    for r in range(M):
        j = xor(m, r)
        w_copies[0, r].wait()
        w_copies[1, r].wait()
        for k in range(E if r else 0):
            c2[r, k].wait_recv()
            for bit in reversed(bits):
                if bit < (r & -r):
                    forward((k, order[k]), r, bit)
        xs = X[j].reshape(E * S, cols)
        gate = gate + jnp.dot(xs, wg[j], preferred_element_type=F32)
        up = up + jnp.dot(xs, wu[j], preferred_element_type=F32)
    hidden = (gate / (1.0 + jnp.exp(-gate)) * up).astype(BF16)

    turns = far_first(E) + [0]
    back = [xor(g, k) for k in turns]
    cr = {}
    cf = []
    for r in reversed(range(M)):
        j = xor(m, r)
        w_copies[2, r].wait()
        part = jnp.dot(hidden, wd[j], preferred_element_type=F32)
        low = r & -r
        if low == 1:
            send_r[r - 1] = part.astype(BF16).reshape(E, S, cols)
        else:
            acc[...] = part.reshape(E, S, cols)
        for k in range(E):
            e = back[k]
            if low != 1:
                total = acc[e]
                for bit in bits:
                    if r & bit:
                        break
                    cr[r + bit, k].wait_recv()
                    if r == 0 and bit == M // 2 and k + W < E:
                        cr[bit, k + W].start()
                    total = total + recv_r[r + bit - 1, e].astype(F32)
                if r:
                    send_r[r - 1, e] = total.astype(BF16)
                else:
                    fin[e] = total.astype(BF16)
            if r:
                c = remote(send_r.at[r - 1, e], recv_r.at[r - 1, e], r_sem, r * E + k,
                           device(g, flip(m, low)))
                if r != M // 2 or k < W:
                    c.start()
                cr[r, k] = c
            elif k < E - 1:
                c = remote(fin.at[e], ret.at[g], f_sem, turns[k], device(e, m))
                c.start()
                cf.append(c)
    ret[g] = fin[g]
    for c in cf:
        c.wait()
    high = high.astype(BF16)
    rest = rest.astype(BF16)
    got = ret[...].reshape(E * S, cols)
    branch = (jnp.dot(high, got, preferred_element_type=F32)
              + jnp.dot(rest, got, preferred_element_type=F32))
    for j in range(M):
        s4[j] = fold(branch[j * rows:(j + 1) * rows], half).astype(BF16)
    c4 = []
    for r in reversed(range(1, M)):
        p = xor(m, r)
        c = remote(s4.at[p], g4.at[m], s4_sem, r, device(g, p))
        c.start()
        c4.append(c)
    g4[m] = s4[m]
    for c in c4:
        c.wait()
    alive = column(live[...])
    for j in range(M):
        span = slice(j * cols, (j + 1) * cols)
        out[:, span] = (states[:, span].astype(F32) + alive * unfold(g4[j].astype(F32), cols)).astype(BF16)
    late = [c1[k] for k in c1 if not E // 2 <= k < E - V]
    for c in late + list(c2.values()) + list(cr.values()):
        c.wait_send()


def body(states, norm_gain, w_gate, w_up, w_down, expert_ids, route_weights, live_rows):
    rows, width = states.shape
    nodes = lax.axis_size("node")
    devc = lax.axis_size("dev")
    E = nodes // SPREAD
    M = SPREAD * devc
    cap = min(rows, rows * expert_ids.shape[1] // E * 2)
    S = cap * M
    cols = width // M
    half = -(-cols // 256) * 128
    hid = w_gate.shape[2]
    vmem = pl.BlockSpec(memory_space=pltpu.VMEM)
    hbm = pl.BlockSpec(memory_space=pl.ANY)
    dma = pltpu.SemaphoreType.DMA
    return pl.pallas_call(
        functools.partial(kernel, E, M, devc),
        out_shape=jax.ShapeDtypeStruct((rows, width), BF16),
        in_specs=[vmem, vmem, hbm, hbm, hbm, vmem, vmem, vmem],
        out_specs=vmem,
        scratch_shapes=[
            pltpu.VMEM((M, cols, hid), BF16),
            pltpu.VMEM((M, cols, hid), BF16),
            pltpu.VMEM((M, hid, cols), BF16),
            pltpu.VMEM((M, 2 * rows, half + E * S), BF16),
            pltpu.VMEM((M, 2 * rows, half + E * S), BF16),
            pltpu.VMEM((E, S, cols), BF16),
            pltpu.VMEM((M, E, S, cols), BF16),
            pltpu.VMEM((E, S, cols), F32),
            pltpu.VMEM((M - 1, E, S, cols), BF16),
            pltpu.VMEM((M - 1, E, S, cols), BF16),
            pltpu.VMEM((E, S, cols), BF16),
            pltpu.VMEM((E, S, cols), BF16),
            pltpu.VMEM((M, 2 * rows, half), BF16),
            pltpu.VMEM((M, 2 * rows, half), BF16),
            dma((3, M)), dma((2, M)), dma((2, E)), dma((2, M * E)), dma((2, M * E)),
            dma((2, E)), dma((2, M)),
        ],
        compiler_params=pltpu.CompilerParams(
            collective_id=0, has_side_effects=True, vmem_limit_bytes=56 * 1024 * 1024),
    )(states, norm_gain.reshape(1, width), w_gate, w_up, w_down, expert_ids.T, route_weights.T,
      live_rows.reshape(1, rows))


def solution(mesh):
    placed = (
        P(("grp", "node", "dev"), None),
        P(),
        P("node", None, "dev"),
        P("node", None, "dev"),
        P("node", "dev", None),
        P(("grp", "node", "dev"), None),
        P(("grp", "node", "dev"), None),
        P(("grp", "node", "dev")),
    )
    return jax.shard_map(
        body, mesh=mesh, in_specs=placed, out_specs=P(("grp", "node", "dev"), None), check_vma=False
    )
```

```python
import functools

import jax
import jax.numpy as jnp
from jax import lax
from jax.experimental import pallas as pl
from jax.experimental.pallas import tpu as pltpu
from jax.sharding import PartitionSpec as P

SPREAD = 4
W = 4
V = 2
norm_eps = 1e-06
F32 = jnp.float32
BF16 = jnp.bfloat16


def flip(value, bit):
    return value + bit - 2 * bit * ((value // bit) % 2)


def xor(value, mask):
    bit = 1
    while bit <= mask:
        if mask & bit:
            value = flip(value, bit)
        bit *= 2
    return value


def fold(value, half):
    rows, cols = value.shape
    second = value[:, half:]
    if cols < 2 * half:
        second = jnp.concatenate([second, jnp.zeros((rows, 2 * half - cols), F32)], axis=1)
    return jnp.concatenate([value[:, :half], second], axis=0)


def unfold(value, cols):
    rows, half = value.shape[0] // 2, value.shape[1]
    return jnp.concatenate([value[:rows], value[rows:, :cols - half]], axis=1)


def far_first(E):
    return list(range(E - 1, 0, -1))


def kernel(E, M, DEVC, states, gain, w_gate, w_up, w_down, ids, route, live, out,
           wg, wu, wd, s0, g0, s1, X, acc, send_r, recv_r, fin, ret, s4, g4,
           w_sem, s0_sem, s1_sem, s2_sem, r_sem, f_sem, s4_sem):
    rows, width = states.shape
    cols = width // M
    S = s1.shape[1]
    cap = S // M
    half = s4.shape[2]
    bits = []
    b = 1
    while b < M:
        bits.append(b)
        b *= 2
    grp = lax.axis_index("grp")
    node = lax.axis_index("node")
    dev = lax.axis_index("dev")
    g = node // SPREAD
    m = (node % SPREAD) * DEVC + dev

    def device(group, member):
        return (grp, group * SPREAD + member // DEVC, member % DEVC)

    def remote(src, dst, sems, at, target):
        return pltpu.make_async_remote_copy(
            src_ref=src, dst_ref=dst, send_sem=sems.at[0, at], recv_sem=sems.at[1, at],
            device_id=target, device_id_type=pl.DeviceIdType.MESH)

    w_copies = {}
    for r in range(M):
        j = xor(m, r)
        span = pl.ds(pl.multiple_of(j * cols, cols), cols)
        w_copies[0, r] = pltpu.make_async_copy(w_gate.at[0, span, :], wg.at[j], w_sem.at[0, r])
        w_copies[1, r] = pltpu.make_async_copy(w_up.at[0, span, :], wu.at[j], w_sem.at[1, r])
        w_copies[2, r] = pltpu.make_async_copy(w_down.at[0, :, span], wd.at[j], w_sem.at[2, r])
    for r in range(M):
        w_copies[0, r].start()
        w_copies[1, r].start()
    for r in reversed(range(M)):
        w_copies[2, r].start()

    barrier = pltpu.get_barrier_semaphore()
    for r in range(1, M):
        pl.semaphore_signal(barrier, inc=1, device_id=device(g, xor(m, r)),
                            device_id_type=pl.DeviceIdType.MESH)
    for k in range(1, E):
        pl.semaphore_signal(barrier, inc=1, device_id=device(xor(g, k), m),
                            device_id_type=pl.DeviceIdType.MESH)

    x = states[...].astype(F32)
    mean_square = jnp.mean(x * x, axis=1, keepdims=True)
    normed = (x * lax.rsqrt(mean_square + norm_eps) * gain[...]).astype(BF16).astype(F32)
    lane = lax.broadcasted_iota(jnp.int32, (rows, E * S), 1)
    row = lax.broadcasted_iota(jnp.int32, (rows, E * S), 0)
    expert = (lane // S).astype(F32)
    diagonal = (lax.broadcasted_iota(jnp.int32, (rows, rows), 0)
                == lax.broadcasted_iota(jnp.int32, (rows, rows), 1))

    def column(line):
        spread = jnp.broadcast_to(line.astype(F32), (rows, rows))
        return jnp.sum(jnp.where(diagonal, spread, 0.0), axis=1, keepdims=True)

    hit_weight = jnp.zeros((rows, E * S), F32)
    hit = jnp.zeros((rows, E * S), jnp.int32)
    for k in range(ids.shape[0]):
        here = column(ids[k:k + 1, :]) == expert
        hit = hit + here.astype(jnp.int32)
        hit_weight = hit_weight + jnp.where(here, column(route[k:k + 1, :]), 0.0)
    rank = jnp.zeros((rows, E * S), jnp.int32)
    for r in range(rows - 1):
        rank = rank + jnp.where(row > r, hit[r:r + 1, :], 0)
    placed = jnp.where(rank + m * cap == lane % S, hit_weight, 0.0)
    high = placed.astype(BF16).astype(F32)
    for j in range(M):
        s0[j, :, :half] = fold(normed[:, j * cols:(j + 1) * cols], half).astype(BF16)
        s0[j, :, half:] = jnp.concatenate([high, placed - high], axis=0).astype(BF16)

    pl.semaphore_wait(barrier, M - 1 + E - 1)

    c0 = []
    for r in reversed(range(1, M)):
        p = xor(m, r)
        c = remote(s0.at[p], g0.at[m], s0_sem, r, device(g, p))
        c.start()
        c0.append(c)
    g0[m] = s0[m]
    for c in c0:
        c.wait()
    got = [g0[r].astype(F32) for r in range(M)]
    high = jnp.concatenate([v[:rows, half:] for v in got], axis=0)
    rest = jnp.concatenate([v[rows:, half:] for v in got], axis=0)
    place = high + rest
    mine = jnp.concatenate([unfold(v[:, :half], cols) for v in got], axis=0).astype(BF16)
    onehot = jnp.where(place > 0, 1.0, 0.0).T.astype(BF16)
    packed = jnp.dot(onehot, mine, preferred_element_type=F32).astype(BF16)
    s1[...] = packed.reshape(E, S, cols)

    c1 = {}
    for k in list(range(E // 2, E)) + list(range(1, E // 2)):
        e = xor(g, k)
        c = remote(s1.at[e], X.at[m, g], s1_sem, k, device(e, m))
        if k < E // 2 + V:
            c.start()
        c1[k] = c
    X[m, g] = s1[g]
    order = [xor(g, k) for k in range(E)]
    c2 = {}

    def forward(block, r, bit):
        j = xor(m, r)
        c = remote(X.at[j, block[1]], X.at[j, block[1]], s2_sem, (r + bit) * E + block[0],
                   device(g, flip(m, bit)))
        c.start()
        c2[r + bit, block[0]] = c

    for k in range(E):
        if k:
            c1[k].wait_recv()
        if k >= E // 2 and k + V < E:
            c1[k].wait_send()
            c1[k + V].start()
        for bit in reversed(bits):
            forward((k, order[k]), 0, bit)
    hid = wg.shape[2]
    gate = jnp.zeros((E * S, hid), F32)
    up = jnp.zeros((E * S, hid), F32)
    for r in range(M):
        j = xor(m, r)
        w_copies[0, r].wait()
        w_copies[1, r].wait()
        for k in range(E if r else 0):
            c2[r, k].wait_recv()
            for bit in reversed(bits):
                if bit < (r & -r):
                    forward((k, order[k]), r, bit)
        xs = X[j].reshape(E * S, cols)
        gate = gate + jnp.dot(xs, wg[j], preferred_element_type=F32)
        up = up + jnp.dot(xs, wu[j], preferred_element_type=F32)
    hidden = (gate / (1.0 + jnp.exp(-gate)) * up).astype(BF16)

    turns = far_first(E) + [0]
    back = [xor(g, k) for k in turns]
    cr = {}
    cf = []
    for r in reversed(range(M)):
        j = xor(m, r)
        w_copies[2, r].wait()
        part = jnp.dot(hidden, wd[j], preferred_element_type=F32)
        low = r & -r
        if low == 1:
            send_r[r - 1] = part.astype(BF16).reshape(E, S, cols)
        else:
            acc[...] = part.reshape(E, S, cols)
        for k in range(E):
            e = back[k]
            if low != 1:
                total = acc[e]
                for bit in bits:
                    if r & bit:
                        break
                    if bit > 1 or k == 0:
                        cr[r + bit, k].wait_recv()
                    if r == 0 and bit == M // 2 and k + W < E:
                        cr[bit, k + W].start()
                    total = total + recv_r[r + bit - 1, e].astype(F32)
                if r:
                    send_r[r - 1, e] = total.astype(BF16)
                else:
                    fin[e] = total.astype(BF16)
            if low == 1:
                if k == 0:
                    c = remote(send_r.at[r - 1], recv_r.at[r - 1], r_sem, r * E, device(g, flip(m, 1)))
                    c.start()
                    cr[r, 0] = c
            elif r:
                c = remote(send_r.at[r - 1, e], recv_r.at[r - 1, e], r_sem, r * E + k,
                           device(g, flip(m, low)))
                if r != M // 2 or k < W:
                    c.start()
                cr[r, k] = c
            elif k < E - 1:
                c = remote(fin.at[e], ret.at[g], f_sem, turns[k], device(e, m))
                c.start()
                cf.append(c)
    ret[g] = fin[g]
    for c in cf:
        c.wait()
    high = high.astype(BF16)
    rest = rest.astype(BF16)
    got = ret[...].reshape(E * S, cols)
    branch = (jnp.dot(high, got, preferred_element_type=F32)
              + jnp.dot(rest, got, preferred_element_type=F32))
    for j in range(M):
        s4[j] = fold(branch[j * rows:(j + 1) * rows], half).astype(BF16)
    c4 = []
    for r in reversed(range(1, M)):
        p = xor(m, r)
        c = remote(s4.at[p], g4.at[m], s4_sem, r, device(g, p))
        c.start()
        c4.append(c)
    g4[m] = s4[m]
    for c in c4:
        c.wait()
    alive = column(live[...])
    for j in range(M):
        span = slice(j * cols, (j + 1) * cols)
        out[:, span] = (states[:, span].astype(F32) + alive * unfold(g4[j].astype(F32), cols)).astype(BF16)
    late = [c1[k] for k in c1 if not E // 2 <= k < E - V]
    for c in late + list(c2.values()) + list(cr.values()):
        c.wait_send()


def body(states, norm_gain, w_gate, w_up, w_down, expert_ids, route_weights, live_rows):
    rows, width = states.shape
    nodes = lax.axis_size("node")
    devc = lax.axis_size("dev")
    E = nodes // SPREAD
    M = SPREAD * devc
    cap = min(rows, rows * expert_ids.shape[1] // E * 2)
    S = cap * M
    cols = width // M
    half = -(-cols // 256) * 128
    hid = w_gate.shape[2]
    vmem = pl.BlockSpec(memory_space=pltpu.VMEM)
    hbm = pl.BlockSpec(memory_space=pl.ANY)
    dma = pltpu.SemaphoreType.DMA
    return pl.pallas_call(
        functools.partial(kernel, E, M, devc),
        out_shape=jax.ShapeDtypeStruct((rows, width), BF16),
        in_specs=[vmem, vmem, hbm, hbm, hbm, vmem, vmem, vmem],
        out_specs=vmem,
        scratch_shapes=[
            pltpu.VMEM((M, cols, hid), BF16),
            pltpu.VMEM((M, cols, hid), BF16),
            pltpu.VMEM((M, hid, cols), BF16),
            pltpu.VMEM((M, 2 * rows, half + E * S), BF16),
            pltpu.VMEM((M, 2 * rows, half + E * S), BF16),
            pltpu.VMEM((E, S, cols), BF16),
            pltpu.VMEM((M, E, S, cols), BF16),
            pltpu.VMEM((E, S, cols), F32),
            pltpu.VMEM((M - 1, E, S, cols), BF16),
            pltpu.VMEM((M - 1, E, S, cols), BF16),
            pltpu.VMEM((E, S, cols), BF16),
            pltpu.VMEM((E, S, cols), BF16),
            pltpu.VMEM((M, 2 * rows, half), BF16),
            pltpu.VMEM((M, 2 * rows, half), BF16),
            dma((3, M)), dma((2, M)), dma((2, E)), dma((2, M * E)), dma((2, M * E)),
            dma((2, E)), dma((2, M)),
        ],
        compiler_params=pltpu.CompilerParams(
            collective_id=0, has_side_effects=True, vmem_limit_bytes=56 * 1024 * 1024),
    )(states, norm_gain.reshape(1, width), w_gate, w_up, w_down, expert_ids.T, route_weights.T,
      live_rows.reshape(1, rows))


def solution(mesh):
    placed = (
        P(("grp", "node", "dev"), None),
        P(),
        P("node", None, "dev"),
        P("node", None, "dev"),
        P("node", "dev", None),
        P(("grp", "node", "dev"), None),
        P(("grp", "node", "dev"), None),
        P(("grp", "node", "dev")),
    )
    return jax.shard_map(
        body, mesh=mesh, in_specs=placed, out_specs=P(("grp", "node", "dev"), None), check_vma=False
    )
```
